512 devices in a mesh: blk: 32 (over z, y_lo), probe: 16 (over y_hi, x, core).
Axes of the slice: x: 4, y: 4 (y_hi: 2, y_lo: 2; y = y_hi * 2 + y_lo), z: 16, core: 2. Of those that a mesh axis runs over, the one named last changes fastest.
Arguments:
- points: bfloat16 [65536, 256], P(('blk', 'probe')), may hold values from -6 to 6, as said below
- inv_length: float32 [256], replicated, may hold values from 0.07 to 0.26
- solution: float32 [64, 65536], P('probe', 'blk'), may hold values from -6 to 6
- residual: float32 [64, 65536], P('probe', 'blk'), may hold values from -53 to 53, as said below
- direction: float32 [64, 65536], P('probe', 'blk'), may hold values from -53 to 53, as said below
Outputs:
- new_solution: float32 [64, 65536], P('probe', 'blk')
- new_residual: float32 [64, 65536], P('probe', 'blk')
- new_direction: float32 [64, 65536], P('probe', 'blk')
The draws below stay inside these ranges and needn't reach their ends.
Inputs may be any that keep to these rules, and one draw needn't show every extreme that they name: real-valued points. `residual`: a real-valued field. `direction`: a real-valued field.
All inputs are finite; a program needn't handle non-finite values.
Results may differ from the reference program's by a relative error of at most 0.0065.
Values may be sent and summed in bfloat16 or wider, within the bound.
No kernel may reach another device: no remote copies, remote signals or barrier semaphores. Data moves between devices by JAX's collectives and lax.ppermute only.
A program may use at most 64 MiB of HBM per device.

```python
import math
import jax
import jax.numpy as jnp
from jax import lax

F = 256
P_SIZE = 64
NB = 2048
N = 65536


def column_scales(key):
    return 0.1 * jnp.exp(jax.random.uniform(key, (P_SIZE, 1), dtype=jnp.float32) * math.log(10.0))


def row_scales(key, rise):
    places = jnp.arange(N, dtype=jnp.float32) / N
    spread = jax.random.uniform(key, (1, N), dtype=jnp.float32) * math.log(3.5)
    return jnp.exp(math.log(rise) * places[None, :] + spread)


def draw_points(key, part):
    key = jax.random.fold_in(key, 13)
    order_key, centre_key, jitter_key, spread_key = jax.random.split(key, 4)
    groups = N // 32 + 1
    member_group = jax.random.permutation(order_key, N) // 32
    centres = jnp.clip(jax.random.normal(centre_key, (groups, F), dtype=jnp.float32), -4.0, 4.0)
    jitter = jnp.clip(jax.random.normal(jitter_key, (N, F), dtype=jnp.float32), -4.0, 4.0)
    spread = 0.05 * jnp.exp(jax.random.uniform(spread_key, (N, 1), dtype=jnp.float32) * math.log(7.0))
    return jnp.clip(centres[member_group] + spread * jitter, -6.0, 6.0).astype(jnp.bfloat16)


def draw_residual(key, part):
    columns = column_scales(key)
    key = jax.random.fold_in(key, 11)
    first, second = jax.random.split(key)
    base = jnp.clip(jax.random.normal(first, (P_SIZE, N), dtype=jnp.float32), -5.0, 5.0)
    rows = row_scales(second, 3.0)
    return base * rows * columns


def draw_direction(key, part):
    columns = column_scales(key)
    key = jax.random.fold_in(key, 12)
    first, second = jax.random.split(key)
    base = jnp.clip(jax.random.normal(first, (P_SIZE, N), dtype=jnp.float32), -5.0, 5.0)
    rows = row_scales(second, 3.0)
    return base * rows * columns


def levels(own_key, dims, cuts, least, largest):
    loudness, own = 1.0, jax.random.fold_in(own_key, 6)
    for axis_at, shards_of in cuts:
        heights = jnp.exp(jax.random.uniform(jax.random.fold_in(own, axis_at), (shards_of,), jnp.float32, least / len(cuts), largest / len(cuts)))
        loudness = loudness * jnp.repeat(heights, dims[axis_at] // shards_of).reshape([-1 if axis == axis_at else 1 for axis in range(len(dims))])
    return loudness


def scatter_about(key, extent, deviation, bound, cuts=(), kind=jnp.bfloat16):
    level = levels(key, extent, cuts, -0.22, 0.18) if cuts else 1.0
    result = jax.random.normal(key, extent, jnp.float32) * deviation * level
    return jnp.minimum(jnp.maximum(result, -bound), bound).astype(kind)


def setup_inputs(seed: int = 0) -> dict:
    splits = jax.random.split(jax.random.key(seed), 6)
    return {
        "points": draw_points(jax.random.fold_in(splits[5], 71), 0),
        "inv_length": jnp.clip(jnp.exp(jax.random.uniform(splits[1], (F,), jnp.float32, math.log(0.07), math.log(0.26))), 0.07, 0.26),
        "solution": scatter_about(splits[2], (P_SIZE, N), 1.0, 6.0, ((0, 16), (1, 32)), jnp.float32),
        "residual": draw_residual(jax.random.fold_in(splits[5], 71), 0),
        "direction": draw_direction(jax.random.fold_in(splits[5], 71), 0),
    }


noise_var = 0.1
epsilon = 1e-06

def kernel_tile(row_pts, col_pts):
    row_norms = lax.optimization_barrier(jnp.sum(jnp.square(row_pts.astype(jnp.float32)), axis=1))
    col_norms = lax.optimization_barrier(jnp.sum(jnp.square(col_pts.astype(jnp.float32)), axis=1))
    inner = jnp.dot(row_pts, col_pts.T, preferred_element_type=jnp.float32)
    squared = jnp.maximum(row_norms[:, None] + col_norms[None, :] - 2.0 * inner, 0.0)
    distance = jnp.sqrt(5.0 * squared)
    return ((1.0 + distance + distance * distance / 3.0) * jnp.exp(-distance)).astype(jnp.bfloat16)

def reference(points, inv_length, solution, residual, direction):
    scaled = (points.astype(jnp.float32) * inv_length[None, :]).astype(jnp.bfloat16)
    low_direction = direction.astype(jnp.bfloat16)
    blocked = scaled.reshape(N // NB, NB, F)
    dir_blocks = jnp.transpose(low_direction.reshape(P_SIZE, N // NB, NB), (1, 0, 2))

    def one_block(col_pts):

        def add_rows(total, item):
            row_pts, row_dir = item
            return (total + jnp.dot(row_dir, kernel_tile(row_pts, col_pts), preferred_element_type=jnp.float32), None)
        total, unused = lax.scan(add_rows, jnp.zeros((P_SIZE, NB), jnp.float32), (blocked, dir_blocks))
        return total
    pieces = lax.map(one_block, blocked)
    image = jnp.transpose(pieces, (1, 0, 2)).reshape(P_SIZE, N) + noise_var * low_direction.astype(jnp.float32)
    old_norm = lax.optimization_barrier(jnp.sum(residual * residual, axis=1))
    curvature = lax.optimization_barrier(jnp.sum(direction * image, axis=1))
    step_len = old_norm / curvature
    new_solution = solution + step_len[:, None] * direction
    new_residual = residual - step_len[:, None] * image
    new_norm = lax.optimization_barrier(jnp.sum(new_residual * new_residual, axis=1))
    new_direction = new_residual + (new_norm / (old_norm + epsilon))[:, None] * direction
    return (new_solution, new_residual, new_direction)
```

```python
import functools
import math

import jax
import jax.numpy as jnp
from jax import lax
from jax.experimental import pallas as pl
from jax.experimental.pallas import tpu as pltpu
from jax.sharding import Mesh, PartitionSpec as P

noise_var = 0.1
epsilon = 1e-06

LOG2E = 1.0 / math.log(2.0)
EXPONENT = -math.sqrt(5.0) * LOG2E
LINEAR = -3.0 * LOG2E
CONSTANT = 3.0 * LOG2E * LOG2E
LEADING = 1.0 / CONSTANT

BLOCK = ("z", "ylo")
PROBE = ("yhi", "x", "core")
PLANE = ("ylo", "yhi", "x", "core")
CHIPS = ("ylo", "yhi", "x")

FEAT = 256
PROBES = 64
OWN_POINTS = 128
OWN_PROBES = 4
PACKED = OWN_POINTS + PROBES * OWN_POINTS // FEAT
COLS = 512
TOGETHER = 2
ROWS = 256
SLICE = 32


def prepare(row_refs, points, norms, dirs):
    at = 0
    for ref in row_refs:
        for chunk in range(ref.shape[0]):
            here = slice(at, at + OWN_POINTS)
            rows = jnp.transpose(ref[chunk, :OWN_POINTS, :].astype(jnp.float32))
            points[:, here] = (rows * -2.0).astype(jnp.bfloat16)
            norms[:, here] = jnp.broadcast_to(
                jnp.sum(rows * rows, axis=0, keepdims=True), (8, OWN_POINTS)
            )
            low = ref[chunk, OWN_POINTS:, :].astype(jnp.float32)
            low = jnp.concatenate(
                [low[:, :OWN_POINTS], low[:, OWN_POINTS:], jnp.zeros((PROBES, OWN_POINTS))]
            )
            dirs[here, :] = jnp.transpose(low).astype(jnp.bfloat16)
            at += OWN_POINTS


def first_kernel(n_sources, *refs):
    row_refs, refs = refs[:n_sources], refs[n_sources:]
    cols, out_ref, col_norms, *scratch = refs

    @pl.loop(0, cols.shape[0] // COLS)
    def _(at):
        here = pl.ds(pl.multiple_of(at * COLS, COLS), COLS)
        wide = cols[here, :].astype(jnp.float32)
        col_norms[here, :] = jnp.broadcast_to(
            jnp.sum(wide * wide, axis=1, keepdims=True), (COLS, 128)
        )

    tiles(row_refs, cols, col_norms, None, out_ref, *scratch)


def next_kernel(n_sources, *refs):
    row_refs, refs = refs[:n_sources], refs[n_sources:]
    cols, col_norms, carry_ref, out_ref, *scratch = refs
    tiles(row_refs, cols, col_norms, carry_ref, out_ref, *scratch)


def tiles(
    row_refs, cols, col_norms, carry_ref, out_ref, points, norms, dirs, inners, values
):
    prepare(row_refs, points, norms, dirs)
    n_rows, n_cols = points.shape[1], cols.shape[0]
    tops = [(top, min(ROWS, n_rows - top)) for top in range(0, n_rows, ROWS)]
    steps = [(left, top, rows) for left in range(TOGETHER) for top, rows in tops]

    def block(at):
        return pl.ds(pl.multiple_of(at * COLS, COLS), COLS)

    def inner(slot, top, rows, here):
        inners[slot, :, :rows] = jnp.dot(
            cols[here, :], points[:, top : top + rows], preferred_element_type=jnp.float32
        )

    def kernel_values(slot, top, rows, at):
        for col in range(0, COLS, SLICE):
            there = pl.ds(pl.multiple_of(at * COLS, COLS) + col, SLICE)
            own_norms = col_norms[there, :]
            for row in range(0, rows, 128):
                squared = inners[slot, col : col + SLICE, row : row + 128] + own_norms
                squared = squared.reshape(SLICE // 8, 8, 128)
                squared = squared + norms[:, top + row : top + row + 128]
                squared = jnp.maximum(squared, 1e-30)
                power = squared * lax.rsqrt(squared) * EXPONENT
                value = ((power + LINEAR) * power + CONSTANT) * jnp.exp2(power)
                values[slot, col : col + SLICE, row : row + 128] = value.reshape(
                    SLICE, 128
                ).astype(jnp.bfloat16)

    def weighted(slot, top, rows):
        return jnp.dot(
            values[slot, :, :rows], dirs[top : top + rows, :], preferred_element_type=jnp.float32
        )

    def finish(at, total):
        if len(out_ref.shape) == 2:
            out_ref[block(at), :] = total
        else:
            width = out_ref.shape[2] // COLS
            groups = PROBES // OWN_PROBES
            total = jnp.transpose(total)[:PROBES] * LEADING
            out_ref[pl.ds(at // width * groups, groups), :, block(at % width)] = total.astype(
                jnp.bfloat16
            ).reshape(groups, OWN_PROBES, COLS)

    last_block = n_cols // COLS - 1
    inner(0, *tops[0], block(0))

    @pl.loop(0, n_cols // (COLS * TOGETHER))
    def _(turn):
        first = turn * TOGETHER

        def add(step, total):
            left, top, rows = steps[step]
            part = weighted(step % 2, top, rows)
            if top:
                part = total + part
            elif carry_ref is not None:
                part = part + carry_ref[block(first + left), :]
            if top + rows == n_rows:
                finish(first + left, part)
            return part

        total = None
        for step, (left, top, rows) in enumerate(steps):
            if step + 1 < len(steps):
                next_left, next_top, next_rows = steps[step + 1]
                inner((step + 1) % 2, next_top, next_rows, block(first + next_left))
            else:
                inner(0, *tops[0], block(jnp.minimum(first + TOGETHER, last_block)))
            kernel_values(step % 2, top, rows, first + left)
            if step:
                total = add(step - 1, total)
        add(len(steps) - 1, total)


WHOLE = pl.BlockSpec(memory_space=pltpu.VMEM)


def product_call(kernel, sources, others, n_cols, out_shape):
    n_rows = sum(source.shape[0] for source in sources) * OWN_POINTS
    return pl.pallas_call(
        functools.partial(kernel, len(sources)),
        in_specs=[WHOLE] * (len(sources) + len(others)),
        out_specs=jax.tree.map(lambda _: WHOLE, out_shape),
        out_shape=out_shape,
        scratch_shapes=[
            pltpu.VMEM((FEAT, n_rows), jnp.bfloat16),
            pltpu.VMEM((8, n_rows), jnp.float32),
            pltpu.VMEM((n_rows, 128), jnp.bfloat16),
            pltpu.VMEM((2, COLS, ROWS), jnp.float32),
            pltpu.VMEM((2, COLS, ROWS), jnp.bfloat16),
        ],
        compiler_params=pltpu.CompilerParams(vmem_limit_bytes=32 * 1024 * 1024),
    )(*sources, *others)


def first_product(sources, cols):
    whole = jax.ShapeDtypeStruct((cols.shape[0], 128), jnp.float32)
    return product_call(first_kernel, sources, [cols], cols.shape[0], [whole, whole])


def tile_product(sources, cols, col_norms, carry, last=False):
    n_cols = cols.shape[0]
    halves = 2
    if last:
        out_shape = jax.ShapeDtypeStruct(
            (halves * PROBES // OWN_PROBES, OWN_PROBES, n_cols // halves), jnp.bfloat16
        )
    else:
        out_shape = jax.ShapeDtypeStruct((n_cols, 128), jnp.float32)
    return product_call(next_kernel, sources, [cols, col_norms, carry], n_cols, out_shape)


def to_all(own, axes):
    return lax.all_to_all(
        jnp.broadcast_to(own[None], (lax.axis_size(axes),) + own.shape),
        axes,
        split_axis=0,
        concat_axis=0,
        tiled=True,
    )


def from_z(shard, by, core_by=None):
    devices = lax.axis_size("z")
    steps = (by, by if core_by is None else core_by)
    pairs = [
        (2 * ((z + steps[core]) % devices) + core, 2 * z + core)
        for z in range(devices)
        for core in range(2)
    ]
    return lax.ppermute(shard, ("z", "core"), pairs)


def shards(points, inv_length, solution, residual, direction):
    own_rows = (points.astype(jnp.float32) * inv_length[None, :]).astype(jnp.bfloat16)
    low_direction = direction.astype(jnp.bfloat16)
    own_dirs = lax.all_to_all(low_direction, PROBE, split_axis=1, concat_axis=0, tiled=True)
    plane_rows, own_dirs = lax.optimization_barrier((own_rows, own_dirs))
    half = PROBES // 2
    packed = jnp.concatenate(
        [own_rows, jnp.concatenate([own_dirs[:half], own_dirs[half:]], axis=1)], axis=0
    )
    first_core = lax.axis_index("core") == 0

    own_half = to_all(plane_rows, CHIPS)

    ahead = from_z(packed, 4)
    behind = from_z(packed, -4)
    own_half, ahead, behind = lax.optimization_barrier((own_half, ahead, behind))
    far = jnp.stack([packed, ahead, behind])
    above = from_z(far, 1)
    below = from_z(far, -1)
    opposite = from_z(jnp.where(first_core, ahead, behind), 4, -4)
    other_half = lax.ppermute(own_half, "core", [(0, 1), (1, 0)])
    cols = jnp.where(
        first_core,
        jnp.stack([own_half, other_half], axis=1),
        jnp.stack([other_half, own_half], axis=1),
    ).reshape(-1, FEAT)
    partial_value, col_norms = first_product([far], cols)

    far, opposite, above, below, partial_value = lax.optimization_barrier(
        (far, opposite[None], above, below, partial_value)
    )
    second = from_z(jnp.concatenate([far, opposite]), 2, -2)
    last_above = from_z(opposite, 1)
    last_below = from_z(opposite, -1)
    partial_value = tile_product([above, below], cols, col_norms, partial_value)
    partial_value = tile_product(
        [opposite, second, last_above, last_below], cols, col_norms, partial_value, last=True
    )
    pieces = lax.all_to_all(partial_value, PLANE, split_axis=0, concat_axis=0, tiled=True)
    image = jnp.sum(pieces.astype(jnp.float32), axis=0) + noise_var * low_direction.astype(
        jnp.float32
    )
    sums = jnp.stack(
        [
            jnp.sum(residual * residual, axis=1),
            jnp.sum(direction * image, axis=1),
            jnp.sum(residual * image, axis=1),
            jnp.sum(image * image, axis=1),
        ]
    )
    sums = jnp.sum(to_all(sums, BLOCK), axis=0)
    old_norm, curvature, cross, image_norm = sums[0], sums[1], sums[2], sums[3]
    step_len = old_norm / curvature
    new_norm = jnp.maximum(old_norm - step_len * (2.0 * cross - step_len * image_norm), 0.0)
    new_solution = solution + step_len[:, None] * direction
    new_residual = residual - step_len[:, None] * image
    new_direction = new_residual + (new_norm / (old_norm + epsilon))[:, None] * direction
    return (new_solution, new_residual, new_direction)


def solution(mesh):
    fine = Mesh(
        mesh.devices.reshape(16, 2, 2, 4, 2), ("z", "ylo", "yhi", "x", "core")
    )
    placed = (P(BLOCK + PROBE, None), P(), P(PROBE, BLOCK), P(PROBE, BLOCK), P(PROBE, BLOCK))
    return jax.shard_map(
        shards,
        mesh=fine,
        in_specs=placed,
        out_specs=(P(PROBE, BLOCK), P(PROBE, BLOCK), P(PROBE, BLOCK)),
        check_vma=False,
    )
```

```python
import functools
import math

import jax
import jax.numpy as jnp
from jax import lax
from jax.experimental import pallas as pl
from jax.experimental.pallas import tpu as pltpu
from jax.sharding import Mesh, PartitionSpec as P

noise_var = 0.1
epsilon = 1e-06

LOG2E = 1.0 / math.log(2.0)
EXPONENT = -math.sqrt(5.0) * LOG2E
LINEAR = -3.0 * LOG2E
CONSTANT = 3.0 * LOG2E * LOG2E
LEADING = 1.0 / CONSTANT

BLOCK = ("z", "ylo")
PROBE = ("yhi", "x", "core")
PLANE = ("ylo", "yhi", "x", "core")

FEAT = 256
PROBES = 64
OWN_POINTS = 128
OWN_PROBES = 4
PACKED = OWN_POINTS + PROBES * OWN_POINTS // FEAT
COLS = 512
TOGETHER = 2
ROWS = 256
SLICE = 32


def prepare(row_refs, points, norms, dirs):
    at = 0
    for ref in row_refs:
        for chunk in range(ref.shape[0]):
            here = slice(at, at + OWN_POINTS)
            rows = jnp.transpose(ref[chunk, :OWN_POINTS, :].astype(jnp.float32))
            points[:, here] = (rows * -2.0).astype(jnp.bfloat16)
            norms[:, here] = jnp.broadcast_to(
                jnp.sum(rows * rows, axis=0, keepdims=True), (8, OWN_POINTS)
            )
            low = ref[chunk, OWN_POINTS:, :].astype(jnp.float32)
            low = jnp.concatenate(
                [low[:, :OWN_POINTS], low[:, OWN_POINTS:], jnp.zeros((PROBES, OWN_POINTS))]
            )
            dirs[here, :] = jnp.transpose(low).astype(jnp.bfloat16)
            at += OWN_POINTS


def first_kernel(n_sources, *refs):
    row_refs, refs = refs[:n_sources], refs[n_sources:]
    cols, out_ref, col_norms, *scratch = refs

    @pl.loop(0, cols.shape[0] // COLS)
    def _(at):
        here = pl.ds(pl.multiple_of(at * COLS, COLS), COLS)
        wide = cols[here, :].astype(jnp.float32)
        col_norms[here, :] = jnp.broadcast_to(
            jnp.sum(wide * wide, axis=1, keepdims=True), (COLS, 128)
        )

    tiles(row_refs, cols, col_norms, None, out_ref, *scratch)


def next_kernel(n_sources, *refs):
    row_refs, refs = refs[:n_sources], refs[n_sources:]
    cols, col_norms, carry_ref, out_ref, *scratch = refs
    tiles(row_refs, cols, col_norms, carry_ref, out_ref, *scratch)


def tiles(
    row_refs, cols, col_norms, carry_ref, out_ref, points, norms, dirs, inners, values
):
    prepare(row_refs, points, norms, dirs)
    n_rows, n_cols = points.shape[1], cols.shape[0]
    tops = [(top, min(ROWS, n_rows - top)) for top in range(0, n_rows, ROWS)]
    steps = [(left, top, rows) for left in range(TOGETHER) for top, rows in tops]

    def block(at):
        return pl.ds(pl.multiple_of(at * COLS, COLS), COLS)

    def inner(slot, top, rows, here):
        inners[slot, :, :rows] = jnp.dot(
            cols[here, :], points[:, top : top + rows], preferred_element_type=jnp.float32
        )

    def kernel_values(slot, top, rows, at):
        for col in range(0, COLS, SLICE):
            there = pl.ds(pl.multiple_of(at * COLS, COLS) + col, SLICE)
            own_norms = col_norms[there, :]
            for row in range(0, rows, 128):
                squared = inners[slot, col : col + SLICE, row : row + 128] + own_norms
                squared = squared.reshape(SLICE // 8, 8, 128)
                squared = squared + norms[:, top + row : top + row + 128]
                squared = jnp.maximum(squared, 1e-30)
                power = squared * lax.rsqrt(squared) * EXPONENT
                value = ((power + LINEAR) * power + CONSTANT) * jnp.exp2(power)
                values[slot, col : col + SLICE, row : row + 128] = value.reshape(
                    SLICE, 128
                ).astype(jnp.bfloat16)

    def weighted(slot, top, rows):
        return jnp.dot(
            values[slot, :, :rows], dirs[top : top + rows, :], preferred_element_type=jnp.float32
        )

    def finish(at, total):
        if len(out_ref.shape) == 2:
            out_ref[block(at), :] = total
        else:
            width = out_ref.shape[2] // COLS
            groups = PROBES // OWN_PROBES
            total = jnp.transpose(total)[:PROBES] * LEADING
            out_ref[pl.ds(at // width * groups, groups), :, block(at % width)] = total.astype(
                jnp.bfloat16
            ).reshape(groups, OWN_PROBES, COLS)

    last_block = n_cols // COLS - 1
    inner(0, *tops[0], block(0))

    @pl.loop(0, n_cols // (COLS * TOGETHER))
    def _(turn):
        first = turn * TOGETHER

        def add(step, total):
            left, top, rows = steps[step]
            part = weighted(step % 2, top, rows)
            if top:
                part = total + part
            elif carry_ref is not None:
                part = part + carry_ref[block(first + left), :]
            if top + rows == n_rows:
                finish(first + left, part)
            return part

        total = None
        for step, (left, top, rows) in enumerate(steps):
            if step + 1 < len(steps):
                next_left, next_top, next_rows = steps[step + 1]
                inner((step + 1) % 2, next_top, next_rows, block(first + next_left))
            else:
                inner(0, *tops[0], block(jnp.minimum(first + TOGETHER, last_block)))
            kernel_values(step % 2, top, rows, first + left)
            if step:
                total = add(step - 1, total)
        add(len(steps) - 1, total)


WHOLE = pl.BlockSpec(memory_space=pltpu.VMEM)


def product_call(kernel, sources, others, n_cols, out_shape):
    n_rows = sum(source.shape[0] for source in sources) * OWN_POINTS
    return pl.pallas_call(
        functools.partial(kernel, len(sources)),
        in_specs=[WHOLE] * (len(sources) + len(others)),
        out_specs=jax.tree.map(lambda _: WHOLE, out_shape),
        out_shape=out_shape,
        scratch_shapes=[
            pltpu.VMEM((FEAT, n_rows), jnp.bfloat16),
            pltpu.VMEM((8, n_rows), jnp.float32),
            pltpu.VMEM((n_rows, 128), jnp.bfloat16),
            pltpu.VMEM((2, COLS, ROWS), jnp.float32),
            pltpu.VMEM((2, COLS, ROWS), jnp.bfloat16),
        ],
        compiler_params=pltpu.CompilerParams(vmem_limit_bytes=32 * 1024 * 1024),
    )(*sources, *others)


def first_product(sources, cols):
    whole = jax.ShapeDtypeStruct((cols.shape[0], 128), jnp.float32)
    return product_call(first_kernel, sources, [cols], cols.shape[0], [whole, whole])


def tile_product(sources, cols, col_norms, carry, last=False):
    n_cols = cols.shape[0]
    halves = 2
    if last:
        out_shape = jax.ShapeDtypeStruct(
            (halves * PROBES // OWN_PROBES, OWN_PROBES, n_cols // halves), jnp.bfloat16
        )
    else:
        out_shape = jax.ShapeDtypeStruct((n_cols, 128), jnp.float32)
    return product_call(next_kernel, sources, [cols, col_norms, carry], n_cols, out_shape)


def copies(own, axes):
    return jnp.broadcast_to(own[None], (lax.axis_size(axes),) + own.shape)


def exchanged(pieces, axes):
    return lax.all_to_all(pieces, axes, split_axis=0, concat_axis=0, tiled=True)


def from_z(shard, by, core_by=None):
    devices = lax.axis_size("z")
    steps = (by, by if core_by is None else core_by)
    pairs = [
        (2 * ((z + steps[core]) % devices) + core, 2 * z + core)
        for z in range(devices)
        for core in range(2)
    ]
    return lax.ppermute(shard, ("z", "core"), pairs)


def shards(points, inv_length, solution, residual, direction):
    own_rows = (points.astype(jnp.float32) * inv_length[None, :]).astype(jnp.bfloat16)
    low_direction = direction.astype(jnp.bfloat16)
    own_dirs = lax.all_to_all(low_direction, PROBE, split_axis=1, concat_axis=0, tiled=True)
    plane_copies, own_dirs = lax.optimization_barrier((copies(own_rows, PLANE), own_dirs))
    half = PROBES // 2
    packed = jnp.concatenate(
        [own_rows, jnp.concatenate([own_dirs[:half], own_dirs[half:]], axis=1)], axis=0
    )
    first_core = lax.axis_index("core") == 0

    cols = exchanged(plane_copies, PLANE).reshape(-1, FEAT)

    ahead = from_z(packed, 4)
    behind = from_z(packed, -4)
    far = jnp.stack([packed, ahead, behind])
    above = from_z(far, 1)
    below = from_z(far, -1)
    opposite = from_z(jnp.where(first_core, ahead, behind), 4, -4)
    partial_value, col_norms = first_product([far], cols)

    far, opposite, above, below, partial_value = lax.optimization_barrier(
        (far, opposite[None], above, below, partial_value)
    )
    second = from_z(jnp.concatenate([far, opposite]), 2, -2)
    last_above = from_z(opposite, 1)
    last_below = from_z(opposite, -1)
    partial_value = tile_product([above, below], cols, col_norms, partial_value)
    partial_value = tile_product(
        [opposite, second, last_above, last_below], cols, col_norms, partial_value, last=True
    )
    pieces = exchanged(partial_value, PLANE)
    image = jnp.sum(pieces.astype(jnp.float32), axis=0) + noise_var * low_direction.astype(
        jnp.float32
    )
    sums = jnp.stack(
        [
            jnp.sum(residual * residual, axis=1),
            jnp.sum(direction * image, axis=1),
            jnp.sum(residual * image, axis=1),
            jnp.sum(image * image, axis=1),
        ]
    )
    sums = jnp.sum(exchanged(copies(sums, BLOCK), BLOCK), axis=0)
    old_norm, curvature, cross, image_norm = sums[0], sums[1], sums[2], sums[3]
    step_len = old_norm / curvature
    new_norm = jnp.maximum(old_norm - step_len * (2.0 * cross - step_len * image_norm), 0.0)
    new_solution = solution + step_len[:, None] * direction
    new_residual = residual - step_len[:, None] * image
    new_direction = new_residual + (new_norm / (old_norm + epsilon))[:, None] * direction
    return (new_solution, new_residual, new_direction)


def solution(mesh):
    fine = Mesh(
        mesh.devices.reshape(16, 2, 2, 4, 2), ("z", "ylo", "yhi", "x", "core")
    )
    placed = (P(BLOCK + PROBE, None), P(), P(PROBE, BLOCK), P(PROBE, BLOCK), P(PROBE, BLOCK))
    return jax.shard_map(
        shards,
        mesh=fine,
        in_specs=placed,
        out_specs=(P(PROBE, BLOCK), P(PROBE, BLOCK), P(PROBE, BLOCK)),
        check_vma=False,
    )
```

```python
import functools
import math

import jax
import jax.numpy as jnp
from jax import lax
from jax.experimental import pallas as pl
from jax.experimental.pallas import tpu as pltpu
from jax.sharding import Mesh, PartitionSpec as P

noise_var = 0.1
epsilon = 1e-06

LOG2E = 1.0 / math.log(2.0)
EXPONENT = -math.sqrt(5.0) * LOG2E
LINEAR = -3.0 * LOG2E
CONSTANT = 3.0 * LOG2E * LOG2E
LEADING = 1.0 / CONSTANT

BLOCK = ("z", "ylo")
PROBE = ("yhi", "x", "core")
PLANE = ("ylo", "yhi", "x", "core")

FEAT = 256
PROBES = 64
OWN_POINTS = 128
OWN_PROBES = 4
PACKED = OWN_POINTS + PROBES * OWN_POINTS // FEAT
COLS = 512
TOGETHER = 2
ROWS = 256
SLICE = 32


def prepare(row_refs, points, norms, dirs):
    at = 0
    for ref in row_refs:
        for chunk in range(ref.shape[0]):
            here = slice(at, at + OWN_POINTS)
            rows = jnp.transpose(ref[chunk, :OWN_POINTS, :].astype(jnp.float32))
            points[:, here] = (rows * -2.0).astype(jnp.bfloat16)
            norms[:, here] = jnp.broadcast_to(
                jnp.sum(rows * rows, axis=0, keepdims=True), (8, OWN_POINTS)
            )
            low = ref[chunk, OWN_POINTS:, :].astype(jnp.float32)
            low = jnp.concatenate(
                [low[:, :OWN_POINTS], low[:, OWN_POINTS:], jnp.zeros((PROBES, OWN_POINTS))]
            )
            dirs[here, :] = jnp.transpose(low).astype(jnp.bfloat16)
            at += OWN_POINTS


def first_kernel(n_sources, *refs):
    row_refs, refs = refs[:n_sources], refs[n_sources:]
    cols, out_ref, col_norms, *scratch = refs

    @pl.loop(0, cols.shape[0] // COLS)
    def _(at):
        here = pl.ds(pl.multiple_of(at * COLS, COLS), COLS)
        wide = cols[here, :].astype(jnp.float32)
        col_norms[here, :] = jnp.broadcast_to(
            jnp.sum(wide * wide, axis=1, keepdims=True), (COLS, 128)
        )

    tiles(row_refs, cols, col_norms, None, out_ref, *scratch)


def next_kernel(n_sources, *refs):
    row_refs, refs = refs[:n_sources], refs[n_sources:]
    cols, col_norms, carry_ref, out_ref, *scratch = refs
    tiles(row_refs, cols, col_norms, carry_ref, out_ref, *scratch)


def tiles(
    row_refs, cols, col_norms, carry_ref, out_ref, points, norms, dirs, inners, values
):
    prepare(row_refs, points, norms, dirs)
    n_rows, n_cols = points.shape[1], cols.shape[0]
    tops = [(top, min(ROWS, n_rows - top)) for top in range(0, n_rows, ROWS)]
    steps = [(left, top, rows) for left in range(TOGETHER) for top, rows in tops]

    def block(at):
        return pl.ds(pl.multiple_of(at * COLS, COLS), COLS)

    def inner(slot, top, rows, here):
        inners[slot, :, :rows] = jnp.dot(
            cols[here, :], points[:, top : top + rows], preferred_element_type=jnp.float32
        )

    def kernel_values(slot, top, rows, at):
        for col in range(0, COLS, SLICE):
            there = pl.ds(pl.multiple_of(at * COLS, COLS) + col, SLICE)
            own_norms = col_norms[there, :]
            for row in range(0, rows, 128):
                squared = inners[slot, col : col + SLICE, row : row + 128] + own_norms
                squared = squared.reshape(SLICE // 8, 8, 128)
                squared = squared + norms[:, top + row : top + row + 128]
                squared = jnp.maximum(squared, 1e-30)
                power = squared * lax.rsqrt(squared) * EXPONENT
                value = ((power + LINEAR) * power + CONSTANT) * jnp.exp2(power)
                values[slot, col : col + SLICE, row : row + 128] = value.reshape(
                    SLICE, 128
                ).astype(jnp.bfloat16)

    def weighted(slot, top, rows):
        return jnp.dot(
            values[slot, :, :rows], dirs[top : top + rows, :], preferred_element_type=jnp.float32
        )

    def finish(at, total):
        if len(out_ref.shape) == 2:
            out_ref[block(at), :] = total
        else:
            width = out_ref.shape[2] // COLS
            groups = PROBES // OWN_PROBES
            total = jnp.transpose(total)[:PROBES] * LEADING
            out_ref[pl.ds(at // width * groups, groups), :, block(at % width)] = total.astype(
                jnp.bfloat16
            ).reshape(groups, OWN_PROBES, COLS)

    last_block = n_cols // COLS - 1
    inner(0, *tops[0], block(0))

    @pl.loop(0, n_cols // (COLS * TOGETHER))
    def _(turn):
        first = turn * TOGETHER

        def add(step, total):
            left, top, rows = steps[step]
            part = weighted(step % 2, top, rows)
            if top:
                part = total + part
            elif carry_ref is not None:
                part = part + carry_ref[block(first + left), :]
            if top + rows == n_rows:
                finish(first + left, part)
            return part

        total = None
        for step, (left, top, rows) in enumerate(steps):
            if step + 1 < len(steps):
                next_left, next_top, next_rows = steps[step + 1]
                inner((step + 1) % 2, next_top, next_rows, block(first + next_left))
            else:
                inner(0, *tops[0], block(jnp.minimum(first + TOGETHER, last_block)))
            kernel_values(step % 2, top, rows, first + left)
            if step:
                total = add(step - 1, total)
        add(len(steps) - 1, total)


WHOLE = pl.BlockSpec(memory_space=pltpu.VMEM)


def product_call(kernel, sources, others, n_cols, out_shape):
    n_rows = sum(source.shape[0] for source in sources) * OWN_POINTS
    return pl.pallas_call(
        functools.partial(kernel, len(sources)),
        in_specs=[WHOLE] * (len(sources) + len(others)),
        out_specs=jax.tree.map(lambda _: WHOLE, out_shape),
        out_shape=out_shape,
        scratch_shapes=[
            pltpu.VMEM((FEAT, n_rows), jnp.bfloat16),
            pltpu.VMEM((8, n_rows), jnp.float32),
            pltpu.VMEM((n_rows, 128), jnp.bfloat16),
            pltpu.VMEM((2, COLS, ROWS), jnp.float32),
            pltpu.VMEM((2, COLS, ROWS), jnp.bfloat16),
        ],
        compiler_params=pltpu.CompilerParams(vmem_limit_bytes=32 * 1024 * 1024),
    )(*sources, *others)


def first_product(sources, cols):
    whole = jax.ShapeDtypeStruct((cols.shape[0], 128), jnp.float32)
    return product_call(first_kernel, sources, [cols], cols.shape[0], [whole, whole])


def tile_product(sources, cols, col_norms, carry, last=False):
    n_cols = cols.shape[0]
    halves = 2
    if last:
        out_shape = jax.ShapeDtypeStruct(
            (halves * PROBES // OWN_PROBES, OWN_PROBES, n_cols // halves), jnp.bfloat16
        )
    else:
        out_shape = jax.ShapeDtypeStruct((n_cols, 128), jnp.float32)
    return product_call(next_kernel, sources, [cols, col_norms, carry], n_cols, out_shape)


def copies(own, axes):
    return jnp.broadcast_to(own[None], (lax.axis_size(axes),) + own.shape)


def exchanged(pieces, axes):
    return lax.all_to_all(pieces, axes, split_axis=0, concat_axis=0, tiled=True)


def from_z(shard, by, core_by=None):
    devices = lax.axis_size("z")
    steps = (by, by if core_by is None else core_by)
    pairs = [
        (2 * ((z + steps[core]) % devices) + core, 2 * z + core)
        for z in range(devices)
        for core in range(2)
    ]
    return lax.ppermute(shard, ("z", "core"), pairs)


def scale_kernel(points_ref, inverse_ref, rows_ref, copies_ref):
    rows = (points_ref[...].astype(jnp.float32) * inverse_ref[...]).astype(jnp.bfloat16)
    rows_ref[...] = rows

    @pl.loop(0, copies_ref.shape[0])
    def _(at):
        copies_ref[at] = rows


def scaled_with_copies(points, inv_length, n_copies):
    return pl.pallas_call(
        scale_kernel,
        in_specs=[WHOLE, WHOLE],
        out_specs=[WHOLE, WHOLE],
        out_shape=[
            jax.ShapeDtypeStruct(points.shape, jnp.bfloat16),
            jax.ShapeDtypeStruct((n_copies,) + points.shape, jnp.bfloat16),
        ],
    )(points, inv_length[None, :])


def shards(points, inv_length, solution, residual, direction):
    own_rows, plane_copies = scaled_with_copies(points, inv_length, lax.axis_size(PLANE))
    low_direction = direction.astype(jnp.bfloat16)
    own_dirs = lax.all_to_all(low_direction, PROBE, split_axis=1, concat_axis=0, tiled=True)
    plane_copies, own_dirs = lax.optimization_barrier((plane_copies, own_dirs))
    half = PROBES // 2
    packed = jnp.concatenate(
        [own_rows, jnp.concatenate([own_dirs[:half], own_dirs[half:]], axis=1)], axis=0
    )
    first_core = lax.axis_index("core") == 0

    cols = exchanged(plane_copies, PLANE).reshape(-1, FEAT)

    ahead = from_z(packed, 4)
    behind = from_z(packed, -4)
    far = jnp.stack([packed, ahead, behind])
    above = from_z(far, 1)
    below = from_z(far, -1)
    opposite = from_z(jnp.where(first_core, ahead, behind), 4, -4)
    partial_value, col_norms = first_product([far], cols)

    far, opposite, above, below, partial_value = lax.optimization_barrier(
        (far, opposite[None], above, below, partial_value)
    )
    second = from_z(jnp.concatenate([far, opposite]), 2, -2)
    last_above = from_z(opposite, 1)
    last_below = from_z(opposite, -1)
    partial_value = tile_product([above, below], cols, col_norms, partial_value)
    partial_value = tile_product(
        [opposite, second, last_above, last_below], cols, col_norms, partial_value, last=True
    )
    pieces = exchanged(partial_value, PLANE)
    image = jnp.sum(pieces.astype(jnp.float32), axis=0) + noise_var * low_direction.astype(
        jnp.float32
    )
    sums = jnp.stack(
        [
            jnp.sum(residual * residual, axis=1),
            jnp.sum(direction * image, axis=1),
            jnp.sum(residual * image, axis=1),
            jnp.sum(image * image, axis=1),
        ]
    )
    sums = jnp.sum(exchanged(copies(sums, BLOCK), BLOCK), axis=0)
    old_norm, curvature, cross, image_norm = sums[0], sums[1], sums[2], sums[3]
    step_len = old_norm / curvature
    new_norm = jnp.maximum(old_norm - step_len * (2.0 * cross - step_len * image_norm), 0.0)
    new_solution = solution + step_len[:, None] * direction
    new_residual = residual - step_len[:, None] * image
    new_direction = new_residual + (new_norm / (old_norm + epsilon))[:, None] * direction
    return (new_solution, new_residual, new_direction)


def solution(mesh):
    fine = Mesh(
        mesh.devices.reshape(16, 2, 2, 4, 2), ("z", "ylo", "yhi", "x", "core")
    )
    placed = (P(BLOCK + PROBE, None), P(), P(PROBE, BLOCK), P(PROBE, BLOCK), P(PROBE, BLOCK))
    return jax.shard_map(
        shards,
        mesh=fine,
        in_specs=placed,
        out_specs=(P(PROBE, BLOCK), P(PROBE, BLOCK), P(PROBE, BLOCK)),
        check_vma=False,
    )
```

```python
import functools
import math

import jax
import jax.numpy as jnp
from jax import lax
from jax.experimental import pallas as pl
from jax.experimental.pallas import tpu as pltpu
from jax.sharding import Mesh, PartitionSpec as P

noise_var = 0.1
epsilon = 1e-06

LOG2E = 1.0 / math.log(2.0)
EXPONENT = -math.sqrt(5.0) * LOG2E
LINEAR = -3.0 * LOG2E
CONSTANT = 3.0 * LOG2E * LOG2E
LEADING = 1.0 / CONSTANT

BLOCK = ("z", "ylo")
PROBE = ("yhi", "x", "core")
PLANE = ("ylo", "yhi", "x", "core")

FEAT = 256
PROBES = 64
OWN_POINTS = 128
OWN_PROBES = 4
PACKED = OWN_POINTS + PROBES * OWN_POINTS // FEAT
COLS = 512
TOGETHER = 2
ROWS = 256
SLICE = 32


def prepare(row_refs, points, norms, dirs):
    at = 0
    for ref in row_refs:
        for chunk in range(ref.shape[0]):
            here = slice(at, at + OWN_POINTS)
            rows = jnp.transpose(ref[chunk, :OWN_POINTS, :].astype(jnp.float32))
            points[:, here] = (rows * -2.0).astype(jnp.bfloat16)
            norms[:, here] = jnp.broadcast_to(
                jnp.sum(rows * rows, axis=0, keepdims=True), (8, OWN_POINTS)
            )
            low = ref[chunk, OWN_POINTS:, :].astype(jnp.float32)
            low = jnp.concatenate(
                [low[:, :OWN_POINTS], low[:, OWN_POINTS:], jnp.zeros((PROBES, OWN_POINTS))]
            )
            dirs[here, :] = jnp.transpose(low).astype(jnp.bfloat16)
            at += OWN_POINTS


def first_kernel(n_sources, *refs):
    row_refs, refs = refs[:n_sources], refs[n_sources:]
    cols, out_ref, col_norms, *scratch = refs

    @pl.loop(0, cols.shape[0] // COLS)
    def _(at):
        here = pl.ds(pl.multiple_of(at * COLS, COLS), COLS)
        wide = cols[here, :].astype(jnp.float32)
        col_norms[here, :] = jnp.broadcast_to(
            jnp.sum(wide * wide, axis=1, keepdims=True), (COLS, 128)
        )

    tiles(row_refs, cols, col_norms, None, out_ref, *scratch)


def next_kernel(n_sources, *refs):
    row_refs, refs = refs[:n_sources], refs[n_sources:]
    cols, col_norms, carry_ref, out_ref, *scratch = refs
    tiles(row_refs, cols, col_norms, carry_ref, out_ref, *scratch)


def tiles(
    row_refs, cols, col_norms, carry_ref, out_ref, points, norms, dirs, inners, values
):
    prepare(row_refs, points, norms, dirs)
    n_rows, n_cols = points.shape[1], cols.shape[0]
    tops = [(top, min(ROWS, n_rows - top)) for top in range(0, n_rows, ROWS)]
    steps = [(left, top, rows) for left in range(TOGETHER) for top, rows in tops]

    def block(at):
        return pl.ds(pl.multiple_of(at * COLS, COLS), COLS)

    def inner(slot, top, rows, here):
        inners[slot, :, :rows] = jnp.dot(
            cols[here, :], points[:, top : top + rows], preferred_element_type=jnp.float32
        )

    def kernel_values(slot, top, rows, at):
        for col in range(0, COLS, SLICE):
            there = pl.ds(pl.multiple_of(at * COLS, COLS) + col, SLICE)
            own_norms = col_norms[there, :]
            for row in range(0, rows, 128):
                squared = inners[slot, col : col + SLICE, row : row + 128] + own_norms
                squared = squared.reshape(SLICE // 8, 8, 128)
                squared = squared + norms[:, top + row : top + row + 128]
                squared = jnp.maximum(squared, 1e-30)
                power = squared * lax.rsqrt(squared) * EXPONENT
                value = ((power + LINEAR) * power + CONSTANT) * jnp.exp2(power)
                values[slot, col : col + SLICE, row : row + 128] = value.reshape(
                    SLICE, 128
                ).astype(jnp.bfloat16)

    def weighted(slot, top, rows):
        return jnp.dot(
            values[slot, :, :rows], dirs[top : top + rows, :], preferred_element_type=jnp.float32
        )

    def finish(at, total):
        if len(out_ref.shape) == 2:
            out_ref[block(at), :] = total
        else:
            width = out_ref.shape[2] // COLS
            groups = PROBES // OWN_PROBES
            total = jnp.transpose(total)[:PROBES] * LEADING
            out_ref[pl.ds(at // width * groups, groups), :, block(at % width)] = total.astype(
                jnp.bfloat16
            ).reshape(groups, OWN_PROBES, COLS)

    last_block = n_cols // COLS - 1
    inner(0, *tops[0], block(0))

    @pl.loop(0, n_cols // (COLS * TOGETHER))
    def _(turn):
        first = turn * TOGETHER

        def add(step, total):
            left, top, rows = steps[step]
            part = weighted(step % 2, top, rows)
            if top:
                part = total + part
            elif carry_ref is not None:
                part = part + carry_ref[block(first + left), :]
            if top + rows == n_rows:
                finish(first + left, part)
            return part

        total = None
        for step, (left, top, rows) in enumerate(steps):
            if step + 1 < len(steps):
                next_left, next_top, next_rows = steps[step + 1]
                inner((step + 1) % 2, next_top, next_rows, block(first + next_left))
            else:
                inner(0, *tops[0], block(jnp.minimum(first + TOGETHER, last_block)))
            kernel_values(step % 2, top, rows, first + left)
            if step:
                total = add(step - 1, total)
        add(len(steps) - 1, total)


WHOLE = pl.BlockSpec(memory_space=pltpu.VMEM)


def product_call(kernel, sources, others, n_cols, out_shape):
    n_rows = sum(source.shape[0] for source in sources) * OWN_POINTS
    return pl.pallas_call(
        functools.partial(kernel, len(sources)),
        in_specs=[WHOLE] * (len(sources) + len(others)),
        out_specs=jax.tree.map(lambda _: WHOLE, out_shape),
        out_shape=out_shape,
        scratch_shapes=[
            pltpu.VMEM((FEAT, n_rows), jnp.bfloat16),
            pltpu.VMEM((8, n_rows), jnp.float32),
            pltpu.VMEM((n_rows, 128), jnp.bfloat16),
            pltpu.VMEM((2, COLS, ROWS), jnp.float32),
            pltpu.VMEM((2, COLS, ROWS), jnp.bfloat16),
        ],
        compiler_params=pltpu.CompilerParams(vmem_limit_bytes=32 * 1024 * 1024),
    )(*sources, *others)


def first_product(sources, cols):
    whole = jax.ShapeDtypeStruct((cols.shape[0], 128), jnp.float32)
    return product_call(first_kernel, sources, [cols], cols.shape[0], [whole, whole])


def tile_product(sources, cols, col_norms, carry, last=False):
    n_cols = cols.shape[0]
    halves = 2
    if last:
        out_shape = jax.ShapeDtypeStruct(
            (halves * PROBES // OWN_PROBES, OWN_PROBES, n_cols // halves), jnp.bfloat16
        )
    else:
        out_shape = jax.ShapeDtypeStruct((n_cols, 128), jnp.float32)
    return product_call(next_kernel, sources, [cols, col_norms, carry], n_cols, out_shape)


def copies(own, axes):
    return jnp.broadcast_to(own[None], (lax.axis_size(axes),) + own.shape)


def exchanged(pieces, axes):
    return lax.all_to_all(pieces, axes, split_axis=0, concat_axis=0, tiled=True)


def from_z(shard, by, core_by=None):
    devices = lax.axis_size("z")
    steps = (by, by if core_by is None else core_by)
    pairs = [
        (2 * ((z + steps[core]) % devices) + core, 2 * z + core)
        for z in range(devices)
        for core in range(2)
    ]
    return lax.ppermute(shard, ("z", "core"), pairs)


def scale_kernel(points_ref, inverse_ref, rows_ref, copies_ref):
    rows = (points_ref[...].astype(jnp.float32) * inverse_ref[...]).astype(jnp.bfloat16)
    rows_ref[...] = rows

    @pl.loop(0, copies_ref.shape[0])
    def _(at):
        copies_ref[at] = rows


def scaled_with_copies(points, inv_length, n_copies):
    return pl.pallas_call(
        scale_kernel,
        in_specs=[WHOLE, WHOLE],
        out_specs=[WHOLE, WHOLE],
        out_shape=[
            jax.ShapeDtypeStruct(points.shape, jnp.bfloat16),
            jax.ShapeDtypeStruct((n_copies,) + points.shape, jnp.bfloat16),
        ],
    )(points, inv_length[None, :])


def shards(points, inv_length, solution, residual, direction):
    own_rows, plane_copies = scaled_with_copies(points, inv_length, lax.axis_size(PLANE))
    low_direction = direction.astype(jnp.bfloat16)
    own_dirs = lax.all_to_all(low_direction, PROBE, split_axis=1, concat_axis=0, tiled=True)
    plane_copies, own_dirs = lax.optimization_barrier((plane_copies, own_dirs))
    half = PROBES // 2
    packed = jnp.concatenate(
        [own_rows, jnp.concatenate([own_dirs[:half], own_dirs[half:]], axis=1)], axis=0
    )

    cols = exchanged(plane_copies, PLANE).reshape(-1, FEAT)

    first_side = from_z(packed, 4, -4)
    other_side = from_z(packed, -4, 4)
    far = jnp.stack([packed, first_side, other_side])
    first_near = from_z(far, 1, -1)
    other_near = from_z(far, -1, 1)
    opposite = from_z(first_side, 4, -4)
    partial_value, col_norms = first_product([far], cols)

    far, opposite, first_near, other_near, partial_value = lax.optimization_barrier(
        (far, opposite[None], first_near, other_near, partial_value)
    )
    second = from_z(jnp.concatenate([far, opposite]), 2, -2)
    first_last = from_z(opposite, 1, -1)
    other_last = from_z(opposite, -1, 1)
    partial_value = tile_product([first_near, other_near], cols, col_norms, partial_value)
    partial_value = tile_product(
        [opposite, second, first_last, other_last], cols, col_norms, partial_value, last=True
    )
    pieces = exchanged(partial_value, PLANE)
    image = jnp.sum(pieces.astype(jnp.float32), axis=0) + noise_var * low_direction.astype(
        jnp.float32
    )
    sums = jnp.stack(
        [
            jnp.sum(residual * residual, axis=1),
            jnp.sum(direction * image, axis=1),
            jnp.sum(residual * image, axis=1),
            jnp.sum(image * image, axis=1),
        ]
    )
    sums = jnp.sum(exchanged(copies(sums, BLOCK), BLOCK), axis=0)
    old_norm, curvature, cross, image_norm = sums[0], sums[1], sums[2], sums[3]
    step_len = old_norm / curvature
    new_norm = jnp.maximum(old_norm - step_len * (2.0 * cross - step_len * image_norm), 0.0)
    new_solution = solution + step_len[:, None] * direction
    new_residual = residual - step_len[:, None] * image
    new_direction = new_residual + (new_norm / (old_norm + epsilon))[:, None] * direction
    return (new_solution, new_residual, new_direction)


def solution(mesh):
    fine = Mesh(
        mesh.devices.reshape(16, 2, 2, 4, 2), ("z", "ylo", "yhi", "x", "core")
    )
    placed = (P(BLOCK + PROBE, None), P(), P(PROBE, BLOCK), P(PROBE, BLOCK), P(PROBE, BLOCK))
    return jax.shard_map(
        shards,
        mesh=fine,
        in_specs=placed,
        out_specs=(P(PROBE, BLOCK), P(PROBE, BLOCK), P(PROBE, BLOCK)),
        check_vma=False,
    )
```

```python
import functools
import math

import jax
import jax.numpy as jnp
from jax import lax
from jax.experimental import pallas as pl
from jax.experimental.pallas import tpu as pltpu
from jax.sharding import Mesh, PartitionSpec as P

noise_var = 0.1
epsilon = 1e-06

LOG2E = 1.0 / math.log(2.0)
EXPONENT = -math.sqrt(5.0) * LOG2E
LINEAR = -3.0 * LOG2E
CONSTANT = 3.0 * LOG2E * LOG2E
LEADING = 1.0 / CONSTANT

BLOCK = ("z", "ylo")
PROBE = ("yhi", "x", "core")
PLANE = ("ylo", "yhi", "x", "core")

FEAT = 256
PROBES = 64
OWN_POINTS = 128
OWN_PROBES = 4
PACKED = OWN_POINTS + PROBES * OWN_POINTS // FEAT
COLS = 512
TOGETHER = 2
ROWS = 256
SLICE = 32


def prepare(row_refs, points, norms, dirs):
    at = 0
    for ref in row_refs:
        for chunk in range(ref.shape[0]):
            here = slice(at, at + OWN_POINTS)
            rows = jnp.transpose(ref[chunk, :OWN_POINTS, :].astype(jnp.float32))
            points[:, here] = (rows * -2.0).astype(jnp.bfloat16)
            norms[:, here] = jnp.broadcast_to(
                jnp.sum(rows * rows, axis=0, keepdims=True), (8, OWN_POINTS)
            )
            low = ref[chunk, OWN_POINTS:, :].astype(jnp.float32)
            low = jnp.concatenate(
                [low[:, :OWN_POINTS], low[:, OWN_POINTS:], jnp.zeros((PROBES, OWN_POINTS))]
            )
            dirs[here, :] = jnp.transpose(low).astype(jnp.bfloat16)
            at += OWN_POINTS


def first_kernel(n_sources, *refs):
    row_refs, refs = refs[:n_sources], refs[n_sources:]
    cols, out_ref, col_norms, *scratch = refs

    @pl.loop(0, cols.shape[0] // COLS)
    def _(at):
        here = pl.ds(pl.multiple_of(at * COLS, COLS), COLS)
        wide = cols[here, :].astype(jnp.float32)
        col_norms[here, :] = jnp.broadcast_to(
            jnp.sum(wide * wide, axis=1, keepdims=True), (COLS, 128)
        )

    tiles(row_refs, cols, col_norms, None, out_ref, *scratch)


def next_kernel(n_sources, *refs):
    row_refs, refs = refs[:n_sources], refs[n_sources:]
    cols, col_norms, carry_ref, out_ref, *scratch = refs
    tiles(row_refs, cols, col_norms, carry_ref, out_ref, *scratch)


def tiles(
    row_refs, cols, col_norms, carry_ref, out_ref, points, norms, dirs, inners, values
):
    prepare(row_refs, points, norms, dirs)
    n_rows, n_cols = points.shape[1], cols.shape[0]
    tops = [(top, min(ROWS, n_rows - top)) for top in range(0, n_rows, ROWS)]
    steps = [(left, top, rows) for left in range(TOGETHER) for top, rows in tops]

    def block(at):
        return pl.ds(pl.multiple_of(at * COLS, COLS), COLS)

    def inner(slot, top, rows, here):
        inners[slot, :, :rows] = jnp.dot(
            cols[here, :], points[:, top : top + rows], preferred_element_type=jnp.float32
        )

    def kernel_values(slot, top, rows, at):
        for col in range(0, COLS, SLICE):
            there = pl.ds(pl.multiple_of(at * COLS, COLS) + col, SLICE)
            own_norms = col_norms[there, :]
            for row in range(0, rows, 128):
                squared = inners[slot, col : col + SLICE, row : row + 128] + own_norms
                squared = squared.reshape(SLICE // 8, 8, 128)
                squared = squared + norms[:, top + row : top + row + 128]
                squared = jnp.maximum(squared, 1e-30)
                power = squared * lax.rsqrt(squared) * EXPONENT
                value = ((power + LINEAR) * power + CONSTANT) * jnp.exp2(power)
                values[slot, col : col + SLICE, row : row + 128] = value.reshape(
                    SLICE, 128
                ).astype(jnp.bfloat16)

    def weighted(slot, top, rows):
        return jnp.dot(
            values[slot, :, :rows], dirs[top : top + rows, :], preferred_element_type=jnp.float32
        )

    def finish(at, total):
        if len(out_ref.shape) == 2:
            out_ref[block(at), :] = total
        else:
            width = out_ref.shape[2] // COLS
            groups = PROBES // OWN_PROBES
            total = jnp.transpose(total)[:PROBES] * LEADING
            out_ref[pl.ds(at // width * groups, groups), :, block(at % width)] = total.astype(
                jnp.bfloat16
            ).reshape(groups, OWN_PROBES, COLS)

    last_block = n_cols // COLS - 1
    inner(0, *tops[0], block(0))

    @pl.loop(0, n_cols // (COLS * TOGETHER))
    def _(turn):
        first = turn * TOGETHER

        def add(step, total):
            left, top, rows = steps[step]
            part = weighted(step % 2, top, rows)
            if top:
                part = total + part
            elif carry_ref is not None:
                part = part + carry_ref[block(first + left), :]
            if top + rows == n_rows:
                finish(first + left, part)
            return part

        total = None
        for step, (left, top, rows) in enumerate(steps):
            if step + 1 < len(steps):
                next_left, next_top, next_rows = steps[step + 1]
                inner((step + 1) % 2, next_top, next_rows, block(first + next_left))
            else:
                inner(0, *tops[0], block(jnp.minimum(first + TOGETHER, last_block)))
            kernel_values(step % 2, top, rows, first + left)
            if step:
                total = add(step - 1, total)
        add(len(steps) - 1, total)


WHOLE = pl.BlockSpec(memory_space=pltpu.VMEM)


def product_call(kernel, sources, others, n_cols, out_shape):
    n_rows = sum(source.shape[0] for source in sources) * OWN_POINTS
    return pl.pallas_call(
        functools.partial(kernel, len(sources)),
        in_specs=[WHOLE] * (len(sources) + len(others)),
        out_specs=jax.tree.map(lambda _: WHOLE, out_shape),
        out_shape=out_shape,
        scratch_shapes=[
            pltpu.VMEM((FEAT, n_rows), jnp.bfloat16),
            pltpu.VMEM((8, n_rows), jnp.float32),
            pltpu.VMEM((n_rows, 128), jnp.bfloat16),
            pltpu.VMEM((2, COLS, ROWS), jnp.float32),
            pltpu.VMEM((2, COLS, ROWS), jnp.bfloat16),
        ],
        compiler_params=pltpu.CompilerParams(vmem_limit_bytes=32 * 1024 * 1024),
    )(*sources, *others)


def first_product(sources, cols):
    whole = jax.ShapeDtypeStruct((cols.shape[0], 128), jnp.float32)
    return product_call(first_kernel, sources, [cols], cols.shape[0], [whole, whole])


def tile_product(sources, cols, col_norms, carry, last=False):
    n_cols = cols.shape[0]
    halves = 2
    if last:
        out_shape = jax.ShapeDtypeStruct(
            (halves * PROBES // OWN_PROBES, OWN_PROBES, n_cols // halves), jnp.bfloat16
        )
    else:
        out_shape = jax.ShapeDtypeStruct((n_cols, 128), jnp.float32)
    return product_call(next_kernel, sources, [cols, col_norms, carry], n_cols, out_shape)


def copies(own, axes):
    return jnp.broadcast_to(own[None], (lax.axis_size(axes),) + own.shape)


def exchanged(pieces, axes):
    return lax.all_to_all(pieces, axes, split_axis=0, concat_axis=0, tiled=True)


def from_z(shard, by, core_by=None):
    devices = lax.axis_size("z")
    steps = (by, by if core_by is None else core_by)
    pairs = [
        (2 * ((z + steps[core]) % devices) + core, 2 * z + core)
        for z in range(devices)
        for core in range(2)
    ]
    return lax.ppermute(shard, ("z", "core"), pairs)


def scale_kernel(points_ref, inverse_ref, rows_ref, copies_ref):
    rows = (points_ref[...].astype(jnp.float32) * inverse_ref[...]).astype(jnp.bfloat16)
    rows_ref[...] = rows

    @pl.loop(0, copies_ref.shape[0])
    def _(at):
        copies_ref[at] = rows


def scaled_with_copies(points, inv_length, n_copies):
    return pl.pallas_call(
        scale_kernel,
        in_specs=[WHOLE, WHOLE],
        out_specs=[WHOLE, WHOLE],
        out_shape=[
            jax.ShapeDtypeStruct(points.shape, jnp.bfloat16),
            jax.ShapeDtypeStruct((n_copies,) + points.shape, jnp.bfloat16),
        ],
    )(points, inv_length[None, :])


def shards(points, inv_length, solution, residual, direction):
    own_rows, plane_copies = scaled_with_copies(points, inv_length, lax.axis_size(PLANE))
    low_direction = direction.astype(jnp.bfloat16)
    own_dirs = lax.all_to_all(low_direction, PROBE, split_axis=1, concat_axis=0, tiled=True)
    plane_copies, own_dirs = lax.optimization_barrier((plane_copies, own_dirs))
    half = PROBES // 2
    packed = jnp.concatenate(
        [own_rows, jnp.concatenate([own_dirs[:half], own_dirs[half:]], axis=1)], axis=0
    )

    cols = exchanged(plane_copies, PLANE).reshape(-1, FEAT)

    first_side = from_z(packed, 4, -4)
    other_side = from_z(packed, -4, 4)
    far = jnp.stack([packed, first_side, other_side])
    first_near = from_z(far, 1, -1)
    other_near = from_z(far, -1, 1)
    opposite = from_z(first_side, 4, -4)
    partial_value, col_norms = first_product([far], cols)

    far, opposite, first_near, other_near, partial_value = lax.optimization_barrier(
        (far, opposite[None], first_near, other_near, partial_value)
    )
    second = from_z(jnp.concatenate([far, opposite]), -2, 2)
    first_last = from_z(opposite, 1, -1)
    other_last = from_z(opposite, -1, 1)
    partial_value = tile_product([first_near, other_near], cols, col_norms, partial_value)
    partial_value = tile_product(
        [opposite, second, first_last, other_last], cols, col_norms, partial_value, last=True
    )
    pieces = exchanged(partial_value, PLANE)
    image = jnp.sum(pieces.astype(jnp.float32), axis=0) + noise_var * low_direction.astype(
        jnp.float32
    )
    sums = jnp.stack(
        [
            jnp.sum(residual * residual, axis=1),
            jnp.sum(direction * image, axis=1),
            jnp.sum(residual * image, axis=1),
            jnp.sum(image * image, axis=1),
        ]
    )
    sums = jnp.sum(exchanged(copies(sums, BLOCK), BLOCK), axis=0)
    old_norm, curvature, cross, image_norm = sums[0], sums[1], sums[2], sums[3]
    step_len = old_norm / curvature
    new_norm = jnp.maximum(old_norm - step_len * (2.0 * cross - step_len * image_norm), 0.0)
    new_solution = solution + step_len[:, None] * direction
    new_residual = residual - step_len[:, None] * image
    new_direction = new_residual + (new_norm / (old_norm + epsilon))[:, None] * direction
    return (new_solution, new_residual, new_direction)


def solution(mesh):
    fine = Mesh(
        mesh.devices.reshape(16, 2, 2, 4, 2), ("z", "ylo", "yhi", "x", "core")
    )
    placed = (P(BLOCK + PROBE, None), P(), P(PROBE, BLOCK), P(PROBE, BLOCK), P(PROBE, BLOCK))
    return jax.shard_map(
        shards,
        mesh=fine,
        in_specs=placed,
        out_specs=(P(PROBE, BLOCK), P(PROBE, BLOCK), P(PROBE, BLOCK)),
        check_vma=False,
    )
```
